256 devices in a mesh: clip: 4 (over y_lo, core), tm: 32 (over x, z), mp: 2 (over y_hi).
Axes of the slice: x: 4, y: 4 (y_hi: 2, y_lo: 2; y = y_hi * 2 + y_lo), z: 8, core: 2. Of those that a mesh axis runs over, the one named last changes fastest.
Arguments:
- video: bfloat16 [128, 576, 1024], P(('clip', 'tm')), parts along dimension 0, may hold values from -6 to 6
- gain_time: float32 [1024], replicated, may hold values from 0.1 to 1.9
- qkv_time: bfloat16 [1024, 3, 1024], P(None, None, 'mp'), may hold values from -2 to 2
- proj_time: bfloat16 [1024, 1024], P('mp'), may hold values from -0.1875 to 0.1875
- gain_space: float32 [1024], replicated, may hold values from 0.1 to 1.9
- qkv_space: bfloat16 [1024, 3, 1024], P(None, None, 'mp'), may hold values from -2 to 2
- proj_space: bfloat16 [1024, 1024], P('mp'), may hold values from -0.1875 to 0.1875
Outputs:
- encoded: bfloat16 [128, 576, 1024], P(('clip', 'tm')), parts along dimension 0
The draws below stay inside these ranges and needn't reach their ends.
There are 4 independent parts, one for each index of `clip`. The reference program is written for one: setup_inputs(seed, part) draws one part's arguments, and reference() takes and returns one part's arrays. A program takes and returns all parts, laid end to end along the dimension named above; an argument that names none is the same for every part. Nothing has to cross between parts.
All inputs are finite; a program needn't handle non-finite values.
Results may differ from the reference program's by a relative error of at most 0.04.
Values may be sent and summed in bfloat16 or wider, within the bound.
No kernel may reach another device: no remote copies, remote signals or barrier semaphores. Data moves between devices by JAX's collectives and lax.ppermute only.
A program may use at most 128 MiB of HBM per device.

```python
import jax
import jax.numpy as jnp
from jax import lax

D = 1024
HEADS = 16
P_SIZE = 576
FRAMES = 32
N_MP = 2


def drawn_weights(key):
    return jnp.clip(jax.random.normal(key, (D, 3, D), jnp.float32) * D ** (-0.5), -2.0, 2.0)


def draw_qkv_time(key, part):
    key = jax.random.fold_in(key, 11)
    return drawn_weights(key).astype(jnp.bfloat16)


def draw_qkv_space(key, part):
    key = jax.random.fold_in(key, 13)
    return drawn_weights(key).astype(jnp.bfloat16)


def shard_levels(key, dims, shards, smallest, largest):
    level, own = 1.0, jax.random.fold_in(key, 6)
    for axis_at, blocks in shards:
        heights = jnp.exp(jax.random.uniform(jax.random.fold_in(own, axis_at), (blocks,), jnp.float32, smallest / len(shards), largest / len(shards)))
        level = level * jnp.repeat(heights, dims[axis_at] // blocks).reshape([-1 if axis == axis_at else 1 for axis in range(len(dims))])
    return level


def centred(rng, extent, scale, reach, pieces=(), dtype=jnp.bfloat16):
    loudness = shard_levels(rng, extent, pieces, -0.22, 0.18) if pieces else 1.0
    drawn = jax.random.normal(rng, extent, jnp.float32) * scale * loudness
    return jnp.minimum(jnp.maximum(drawn, -reach), reach).astype(dtype)


def setup_inputs(seed: int = 0, part: int = 0) -> dict:
    arg_keys = jax.random.split(jax.random.key(seed), 8)
    part_splits = jax.random.split(jax.random.fold_in(arg_keys[7], part), 8)
    return {
        "video": centred(part_splits[0], (FRAMES, P_SIZE, D), 1.0, 6.0, ((0, 32),)),
        "gain_time": jnp.clip(1.0 + 0.18 * jax.random.normal(arg_keys[1], (D,), jnp.float32), 0.1, 1.9),
        "qkv_time": draw_qkv_time(jax.random.fold_in(arg_keys[7], 71), part),
        "proj_time": centred(arg_keys[3], (D, D), D ** -0.5, 0.1875, ((0, 2),)),
        "gain_space": jnp.clip(1.0 + 0.18 * jax.random.normal(arg_keys[4], (D,), jnp.float32), 0.1, 1.9),
        "qkv_space": draw_qkv_space(jax.random.fold_in(arg_keys[7], 71), part),
        "proj_space": centred(arg_keys[6], (D, D), D ** -0.5, 0.1875, ((0, 2),)),
    }


def layer_norm(values, gain):
    wide = values.astype(jnp.float32)
    center = lax.optimization_barrier(jnp.mean(wide, axis=-1, keepdims=True))
    spread = lax.optimization_barrier(jnp.mean((wide - center) ** 2, axis=-1, keepdims=True))
    return ((wide - center) * lax.rsqrt(spread + 1e-05) * gain).astype(jnp.bfloat16)

def project(normed, weights):
    width = normed.shape[-1]
    lead = normed.shape[:-1]
    flat = jnp.dot(normed.reshape(-1, width), weights.reshape(width, 3 * width), preferred_element_type=jnp.float32)
    return flat.astype(jnp.bfloat16).reshape(lead + (3, HEADS, width // HEADS))

def temporal(query, keys, values):
    scale = 1.0 / jnp.sqrt(jnp.float32(query.shape[-1]))
    q_all = jnp.transpose(query, (1, 0, 2, 3))
    k_all = jnp.transpose(keys, (1, 0, 2, 3))
    v_all = jnp.transpose(values, (1, 0, 2, 3))

    def one_patch(triple):
        q_one, k_one, v_one = triple
        scores = jnp.einsum('fhd,ghd->hfg', q_one.astype(jnp.float32), k_one.astype(jnp.float32)) * scale
        weights = jax.nn.softmax(scores, axis=-1).astype(jnp.bfloat16)
        return jnp.einsum('hfg,ghd->fhd', weights.astype(jnp.float32), v_one.astype(jnp.float32)).astype(jnp.bfloat16)
    result = lax.map(one_patch, (q_all, k_all, v_all))
    return jnp.transpose(result, (1, 0, 2, 3))

def spatial(query, keys, values):
    scale = 1.0 / jnp.sqrt(jnp.float32(query.shape[-1]))

    def one_frame(triple):
        q_one, k_one, v_one = triple
        scores = jnp.einsum('phd,qhd->hpq', q_one.astype(jnp.float32), k_one.astype(jnp.float32)) * scale
        weights = jax.nn.softmax(scores, axis=-1).astype(jnp.bfloat16)
        return jnp.einsum('hpq,qhd->phd', weights.astype(jnp.float32), v_one.astype(jnp.float32)).astype(jnp.bfloat16)
    return lax.map(one_frame, (query, keys, values))

def add_projection(stream, attended, weights):
    width = stream.shape[-1]
    flat = attended.reshape(-1, width)
    group = width // N_MP
    total = jnp.zeros((flat.shape[0], width), jnp.float32)
    for member in range(N_MP):
        partial_sum = jnp.dot(flat[:, member * group:(member + 1) * group], weights[member * group:(member + 1) * group], preferred_element_type=jnp.float32)
        rounded = lax.optimization_barrier(partial_sum.astype(jnp.bfloat16))
        total = total + rounded.astype(jnp.float32)
    return (stream.astype(jnp.float32) + total.reshape(stream.shape)).astype(jnp.bfloat16)

def reference(video, gain_time, qkv_time, proj_time, gain_space, qkv_space, proj_space):
    triple = project(layer_norm(video, gain_time), qkv_time)
    attended = temporal(triple[:, :, 0], triple[:, :, 1], triple[:, :, 2])
    middle = add_projection(video, attended, proj_time)
    triple = project(layer_norm(middle, gain_space), qkv_space)
    attended = spatial(triple[:, :, 0], triple[:, :, 1], triple[:, :, 2])
    return add_projection(middle, attended, proj_space)
```

```python
import functools
import math

import jax
import jax.numpy as jnp
from jax import lax
from jax.experimental import pallas as pl
from jax.experimental.pallas import tpu as pltpu
from jax.sharding import PartitionSpec as P

HD = 64
LANES = 128
ROWS = 8
F32 = jnp.float32
BF16 = jnp.bfloat16
SCALE = math.log2(math.e) / math.sqrt(HD)
EPS = 1e-05
MASKED = -1e30


def dot(left, right):
    return jnp.dot(left, right, preferred_element_type=F32)


def dot_t(left, right):
    return lax.dot_general(left, right, (((1,), (1,)), ((), ())), preferred_element_type=F32)


def iota(shape, dim):
    return lax.broadcasted_iota(jnp.int32, shape, dim)


def layer_norm(wide, gain):
    center = jnp.mean(wide, axis=-1, keepdims=True)
    moved = wide - center
    spread = jnp.mean(moved * moved, axis=-1, keepdims=True)
    return (moved * lax.rsqrt(spread + EPS) * gain).astype(BF16)


def spread_rows(rows):
    n, width = rows.shape
    groups = width // LANES
    at = iota((n * groups, n), 0)
    row = iota((n * groups, n), 1)
    total = jnp.zeros((n * groups, LANES), F32)
    for group in range(groups):
        pick = jnp.where(at == row * groups + group, 1.0, 0.0).astype(BF16)
        total = total + dot(pick, rows[:, group * LANES : (group + 1) * LANES])
    return total


def gather_rows(spread, groups):
    n = spread.shape[0] // groups
    row = iota((n, n * groups), 0)
    at = iota((n, n * groups), 1)
    parts = []
    for group in range(groups):
        pick = jnp.where(at == row * groups + group, 1.0, 0.0).astype(BF16)
        parts.append(dot(pick, spread).astype(BF16))
    return jnp.concatenate(parts, axis=1)


def store_packed(out_ref, main, extra):
    n, rows, _ = out_ref.shape
    width = main.shape[1]
    out_ref[:, :, :width] = main.reshape(n, rows, width).astype(BF16)
    out_ref[:, :, width:] = spread_rows(extra).reshape(n, rows, LANES).astype(BF16)


def load_packed(ref):
    n, rows, full = ref.shape
    width = full - LANES
    main = ref[:, :, :width].astype(F32).reshape(n * rows, width).astype(BF16)
    tail = ref[:, :, width:].astype(F32).reshape(n * rows, LANES).astype(BF16)
    return main, gather_rows(tail, rows)


def half_rows(count, mine):
    member = lax.axis_index("mp")
    place = member if mine else 1 - member
    return pl.ds(pl.multiple_of(place * count, 32), count)


def norm_kernel(x_ref, gain_ref, out_ref):
    half = x_ref.shape[0] // 2
    frames = out_ref.shape[0]
    x = x_ref[half_rows(half, True), :].astype(F32)
    normed = layer_norm(x, gain_ref[...])
    main = frames * ROWS
    store_packed(out_ref, normed[:main].astype(F32), normed[main:])


def place_pieces(pieces, target):
    clip = lax.axis_index("clip")
    count = len(pieces) // 4
    rows = target.shape[-2] // len(pieces)
    for distance in range(4):
        quarter = clip ^ distance
        for chunk in range(count):
            start = pl.multiple_of((quarter * count + chunk) * rows, rows)
            piece = pieces[distance * count + chunk]
            if len(target.shape) == 3:
                target[:, pl.ds(start, rows), :] = piece[...]
            else:
                target[pl.ds(start, rows), :] = piece[...]


def temporal_pairs(q, k, v, out, at, frames):
    rows = q.shape[0]
    block = 4 * frames
    low = iota((block, LANES), 1) < HD
    for pair in range(q.shape[1] // LANES):
        lanes = slice(pair * LANES, (pair + 1) * LANES)
        for start in range(0, rows, block):
            count = min(block, rows - start)
            key_at = start + count - block
            keys = k[key_at : key_at + block, lanes]
            vals = v[key_at : key_at + block, lanes]
            zero = jnp.zeros_like(keys)
            keys2 = jnp.concatenate([jnp.where(low, keys, zero), jnp.where(low, zero, keys)], axis=0)
            vals2 = jnp.concatenate([jnp.where(low, vals, zero), jnp.where(low, zero, vals)], axis=0)
            scores = dot_t(q[start : start + count, lanes], keys2)
            own = (iota((count, 2 * block), 0) + (start - key_at)) // frames
            other = (iota((count, 2 * block), 1) % block) // frames
            scores = jnp.where(own == other, scores, MASKED)
            first = scores[:, :block]
            second = scores[:, block:]
            e_first = jnp.exp2(first - jnp.max(first, axis=-1, keepdims=True))
            e_second = jnp.exp2(second - jnp.max(second, axis=-1, keepdims=True))
            weights = jnp.concatenate([e_first, e_second], axis=1).astype(BF16)
            r_first = 1.0 / jnp.sum(e_first, axis=-1, keepdims=True)
            r_second = 1.0 / jnp.sum(e_second, axis=-1, keepdims=True)
            result = dot(weights, vals2) * jnp.where(low[:count], r_first, r_second)
            out[start : start + count, at + pair * LANES : at + (pair + 1) * LANES] = result.astype(BF16)


def temporal_kernel(count, *refs):
    a_ref, own_ref = refs[:2]
    pieces = refs[2 : 2 + count]
    out_ref, other_ref, att_ref = refs[2 + count :]
    frames = a_ref.shape[0]
    local = own_ref.shape[-1]
    main, extra = load_packed(a_ref)
    size = main.shape[0]
    row = iota((size, size), 0)
    col = iota((size, size), 1)
    swap = jnp.where((row % frames) * ROWS + row // frames == col, 1.0, 0.0).astype(BF16)
    x = jnp.concatenate([dot(swap, main).astype(BF16), extra], axis=0)
    place_pieces(pieces, other_ref)
    for member, weights in enumerate((own_ref, other_ref)):
        q = (dot(x, weights[0]) * SCALE).astype(BF16)
        k = dot(x, weights[1]).astype(BF16)
        v = dot(x, weights[2]).astype(BF16)
        temporal_pairs(q, k, v, att_ref, member * local, frames)
    back = jnp.where((col % frames) * ROWS + col // frames == row, 1.0, 0.0).astype(BF16)
    store_packed(out_ref, dot(back, att_ref[:size, :]), att_ref[size:, :])


def middle_kernel(mine, count, *refs):
    r_ref, x_ref, own_ref = refs[:3]
    pieces = refs[3 : 3 + count]
    gain_ref, w_ref, mid_ref, qkv_ref, other_ref = refs[3 + count :]
    half = x_ref.shape[0] // 2
    place_pieces(pieces, other_ref)
    main, extra = load_packed(r_ref)
    att = jnp.concatenate([main, extra], axis=0)
    local = own_ref.shape[0]
    first, second = (own_ref, other_ref) if mine else (other_ref, own_ref)
    summed = dot(att[:, :local], first[...]) + dot(att[:, local:], second[...])
    mid = (x_ref[half_rows(half, mine), :].astype(F32) + summed).astype(BF16)
    mid_ref[...] = mid
    normed = layer_norm(mid.astype(F32), gain_ref[...])
    qkv_ref[0] = (dot(normed, w_ref[0]) * SCALE).astype(BF16)
    qkv_ref[1] = dot(normed, w_ref[1]).astype(BF16)
    qkv_ref[2] = dot(normed, w_ref[2]).astype(BF16)


def spatial_kernel(first, last, own_ref, other_ref, out_ref):
    half = own_ref.shape[1]
    low = iota((2 * half, LANES), 1) < HD
    for pair in range(first, last):
        lanes = slice(pair * LANES, (pair + 1) * LANES)
        keys = jnp.concatenate([own_ref[1, :, lanes], other_ref[1, :, lanes]], axis=0)
        vals = jnp.concatenate([own_ref[2, :, lanes], other_ref[2, :, lanes]], axis=0)
        zero = jnp.zeros_like(keys)
        one = jnp.ones_like(keys)
        keys_of = (jnp.where(low, keys, zero), jnp.where(low, zero, keys))
        vals_of = (jnp.where(low, vals, one), jnp.where(low, one, vals))
        for part, ref in enumerate((own_ref, other_ref)):
            q = ref[0, :, lanes]
            results = []
            for head in range(2):
                scores = dot_t(q, keys_of[head])
                weights = jnp.exp2(scores - jnp.max(scores, axis=-1, keepdims=True)).astype(BF16)
                results.append(dot(weights, vals_of[head]))
            here = low[:half]
            top = jnp.where(here, results[0], results[1])
            bottom = pltpu.roll(jnp.where(here, results[1], results[0]), HD, 1)
            at = (pair - first) * LANES
            out_ref[part * half : (part + 1) * half, at : at + LANES] = (top / bottom).astype(BF16)


def final_kernel(count, parts, *refs):
    mids = refs[:2]
    own = refs[2 : 2 + parts]
    partner = refs[2 + parts : 2 + 2 * parts]
    own_ref = refs[2 + 2 * parts]
    pieces = refs[3 + 2 * parts : 3 + 2 * parts + count]
    out_ref, other_ref = refs[3 + 2 * parts + count :]
    half = mids[0].shape[0]
    place_pieces(pieces, other_ref)
    for part, mine in enumerate((True, False)):
        here = slice(part * half, (part + 1) * half)
        there = slice((1 - part) * half, (2 - part) * half)
        total = mids[part][...].astype(F32)
        left = jnp.concatenate([ref[here, :] for ref in own], axis=1)
        right = jnp.concatenate([ref[there, :] for ref in partner], axis=1)
        total = total + dot(left, own_ref[...]) + dot(right, other_ref[...])
        out_ref[half_rows(half, mine), :] = total.astype(BF16)


def call(kernel, out, scratch=(), flops=0, limit=32):
    return pl.pallas_call(
        kernel,
        out_shape=out,
        scratch_shapes=list(scratch),
        compiler_params=pltpu.CompilerParams(vmem_limit_bytes=limit * 1024 * 1024),
        cost_estimate=pl.CostEstimate(flops=flops, bytes_accessed=4000000, transcendentals=0),
    )


def shape(*dims):
    return jax.ShapeDtypeStruct(dims, BF16)


def routes():
    devices = [(y, c, m) for y in (0, 1) for c in (0, 1) for m in (0, 1)]

    def index(y, c, m):
        return y * 4 + c * 2 + m

    across = [(index(y, c, m), index(1 - y, c, 1 - m)) for y, c, m in devices]
    beside = [(index(y, c, m), index(1 - y, c, m)) for y, c, m in devices]
    core = [(index(y, c, m), index(y, 1 - c, m)) for y, c, m in devices]
    return across, beside, core


def fetch_other(slices):
    across, beside, core = routes()
    axes = ("clip", "mp")
    mine = [lax.ppermute(piece, axes, across) for piece in slices]
    chip = [lax.ppermute(piece, axes, beside) for piece in mine]
    pair = [lax.ppermute(piece, axes, core) for piece in mine]
    last = [lax.ppermute(piece, axes, core) for piece in chip]
    return mine + pair + chip + last


def cut(weights, chunks):
    quarter = lax.axis_index("clip") ^ 2
    rows = weights.shape[-2] // (4 * chunks)
    lead = weights.ndim - 2
    out = []
    for chunk in range(chunks):
        start = [0] * lead + [(quarter * chunks + chunk) * rows, 0]
        out.append(lax.dynamic_slice(weights, start, weights.shape[:lead] + (rows, weights.shape[-1])))
    return out


def all_to_all(values):
    return lax.all_to_all(values, "tm", split_axis=0, concat_axis=0, tiled=True)


def shards(video, gain_time, qkv_time, proj_time, gain_space, qkv_space, proj_space):
    _, patches, width = video.shape
    frames = lax.axis_size("tm")
    local = qkv_time.shape[-1]
    half = patches // 2
    x = video[0]
    w_time = jnp.transpose(qkv_time, (1, 0, 2))
    w_space = jnp.transpose(qkv_space, (1, 0, 2))
    gain_time = gain_time.reshape(1, width)
    gain_space = gain_space.reshape(1, width)
    packed = shape(frames, ROWS, width + LANES)

    pieces = fetch_other(cut(w_time, 2))
    sent = call(norm_kernel, packed)(x, gain_time)
    arrived = all_to_all(sent)
    *pieces, arrived = lax.optimization_barrier((*pieces, arrived))

    attended = call(
        functools.partial(temporal_kernel, len(pieces)),
        packed,
        [pltpu.VMEM((3, width, local), BF16), pltpu.VMEM((half, width), BF16)],
        flops=2 * half * width * 3 * width,
    )(arrived, w_time, *pieces)
    proj_time_, proj_space_, _ = lax.optimization_barrier((proj_time, proj_space, pieces[-1]))
    time_pieces = fetch_other(cut(proj_time_, 1))
    space_pieces = fetch_other(cut(proj_space_, 1))
    back = all_to_all(attended)
    *both, back = lax.optimization_barrier((*time_pieces, *space_pieces, back))
    time_pieces, space_pieces = both[:4], both[4:]

    theirs = lax.ppermute(back, "mp", [(0, 1), (1, 0)])
    made = []
    for mine, values in ((True, back), (False, theirs)):
        made.append(
            call(
                functools.partial(middle_kernel, mine, 4),
                (shape(half, width), shape(3, half, local)),
                [pltpu.VMEM((local, width), BF16)],
                flops=2 * half * width * 4 * local,
            )(values, x, proj_time, *time_pieces, gain_space, w_space)
        )
    (mid_own, qkv_own), (mid_other, qkv_other) = made

    own, partner = [], []
    pairs = local // LANES
    for first in range(0, pairs, 2):
        part = call(
            functools.partial(spatial_kernel, first, first + 2),
            shape(patches, 2 * LANES),
            flops=4 * patches * patches * 2 * LANES,
        )(qkv_own, qkv_other)
        own.append(part)
        partner.append(lax.ppermute(part, "mp", [(0, 1), (1, 0)]))
    out = call(
        functools.partial(final_kernel, 4, len(own)),
        shape(patches, width),
        [pltpu.VMEM((local, width), BF16)],
        flops=2 * patches * width * width,
    )(mid_own, mid_other, *own, *partner, proj_space, *space_pieces)
    return out[None]


def solution(mesh):
    placed = (
        P(("clip", "tm"), None, None),
        P(),
        P(None, None, "mp"),
        P("mp", None),
        P(),
        P(None, None, "mp"),
        P("mp", None),
    )
    return jax.shard_map(
        shards, mesh=mesh, in_specs=placed, out_specs=P(("clip", "tm"), None, None), check_vma=False
    )
```

```python
import functools
import math

import jax
import jax.numpy as jnp
from jax import lax
from jax.experimental import pallas as pl
from jax.experimental.pallas import tpu as pltpu
from jax.sharding import PartitionSpec as P

HD = 64
LANES = 128
ROWS = 8
F32 = jnp.float32
BF16 = jnp.bfloat16
SCALE = math.log2(math.e) / math.sqrt(HD)
EPS = 1e-05
MASKED = -1e30
C_NORM = 4
C_JOIN = 4


def dot(left, right):
    return jnp.dot(left, right, preferred_element_type=F32)


def dot_t(left, right):
    return lax.dot_general(left, right, (((1,), (1,)), ((), ())), preferred_element_type=F32)


def iota(shape, dim):
    return lax.broadcasted_iota(jnp.int32, shape, dim)


def layer_norm(wide, gain):
    center = jnp.mean(wide, axis=-1, keepdims=True)
    moved = wide - center
    spread = jnp.mean(moved * moved, axis=-1, keepdims=True)
    return (moved * lax.rsqrt(spread + EPS) * gain).astype(BF16)


def spread_rows(rows):
    n, width = rows.shape
    groups = width // LANES
    at = iota((n * groups, n), 0)
    row = iota((n * groups, n), 1)
    total = jnp.zeros((n * groups, LANES), F32)
    for group in range(groups):
        pick = jnp.where(at == row * groups + group, 1.0, 0.0).astype(BF16)
        total = total + dot(pick, rows[:, group * LANES : (group + 1) * LANES])
    return total


def gather_rows(spread, groups):
    n = spread.shape[0] // groups
    row = iota((n, n * groups), 0)
    at = iota((n, n * groups), 1)
    parts = []
    for group in range(groups):
        pick = jnp.where(at == row * groups + group, 1.0, 0.0).astype(BF16)
        parts.append(dot(pick, spread).astype(BF16))
    return jnp.concatenate(parts, axis=1)


def store_packed(out_ref, main, extra):
    n, rows, _ = out_ref.shape
    width = main.shape[1]
    out_ref[:, :, :width] = main.reshape(n, rows, width).astype(BF16)
    out_ref[:, :, width:] = spread_rows(extra).reshape(n, rows, LANES).astype(BF16)


def load_packed(ref):
    n, rows, full = ref.shape
    width = full - LANES
    main = ref[:, :, :width].astype(F32).reshape(n * rows, width).astype(BF16)
    tail = ref[:, :, width:].astype(F32).reshape(n * rows, LANES).astype(BF16)
    return main, gather_rows(tail, rows)


def half_rows(count, mine):
    member = lax.axis_index("mp")
    place = member if mine else 1 - member
    return pl.ds(pl.multiple_of(place * count, 32), count)


def cut_kernel(w_ref, out_ref, sem):
    rows = out_ref.shape[1]
    start = (lax.axis_index("clip") ^ 2) * rows
    copy = pltpu.make_async_copy(w_ref.at[:, pl.ds(pl.multiple_of(start, 16), rows), :], out_ref, sem)
    copy.start()
    copy.wait()


def cut_proj_kernel(time_ref, space_ref, time_out, space_out, sems):
    rows = time_out.shape[0]
    start = (lax.axis_index("clip") ^ 2) * rows
    place = pl.ds(pl.multiple_of(start, rows), rows)
    copies = [
        pltpu.make_async_copy(time_ref.at[place, :], time_out, sems.at[0]),
        pltpu.make_async_copy(space_ref.at[place, :], space_out, sems.at[1]),
    ]
    for copy in copies:
        copy.start()
    for copy in copies:
        copy.wait()


def norm_kernel(x_ref, gain_ref, w_ref, out_ref, cut_ref, held, gain, sems):
    half = held.shape[0]
    main = out_ref.shape[0] * ROWS
    rows = cut_ref.shape[1]
    start = w_ref.shape[1] - 2 * rows + (lax.axis_index("clip") % 2) * rows
    place = pl.ds(pl.multiple_of(start, 16), rows)
    copies = [
        pltpu.make_async_copy(x_ref.at[half_rows(half, True), :], held, sems.at[0]),
        pltpu.make_async_copy(gain_ref, gain, sems.at[1]),
        pltpu.make_async_copy(w_ref.at[:, place, :], cut_ref, sems.at[2]),
    ]
    for copy in copies:
        copy.start()
    copies[0].wait()
    copies[1].wait()
    normed = layer_norm(held[...].astype(F32), gain[...])
    store_packed(out_ref, normed[:main].astype(F32), normed[main:])
    copies[2].wait()


def piece_copies(pieces, starts, target, sems):
    copies = []
    for at, (piece, start) in enumerate(zip(pieces, starts, strict=True)):
        place = pl.ds(pl.multiple_of(start, 16), piece.shape[-2])
        spot = target.at[:, place, :] if len(target.shape) == 3 else target.at[place, :]
        copies.append(pltpu.make_async_copy(piece, spot, sems.at[at]))
    return copies


def part_starts(first, second):
    clip = lax.axis_index("clip")
    starts = [(clip ^ distance) * first for distance in range(4)]
    return starts + [4 * first + ((clip % 2) ^ distance) * second for distance in range(2)]


def quarter_starts(rows):
    clip = lax.axis_index("clip")
    return [(clip ^ distance) * rows for distance in range(4)]


def temporal_pairs(q, k, v, out, at, frames):
    rows = q.shape[0]
    block = 4 * frames
    low = iota((block, LANES), 1) < HD
    for pair in range(q.shape[1] // LANES):
        lanes = slice(pair * LANES, (pair + 1) * LANES)
        for start in range(0, rows, block):
            count = min(block, rows - start)
            key_at = start + count - block
            keys = k[key_at : key_at + block, lanes]
            vals = v[key_at : key_at + block, lanes]
            zero = jnp.zeros_like(keys)
            keys2 = jnp.concatenate([jnp.where(low, keys, zero), jnp.where(low, zero, keys)], axis=0)
            vals2 = jnp.concatenate([jnp.where(low, vals, zero), jnp.where(low, zero, vals)], axis=0)
            scores = dot_t(q[start : start + count, lanes], keys2)
            own = (iota((count, 2 * block), 0) + (start - key_at)) // frames
            other = (iota((count, 2 * block), 1) % block) // frames
            scores = jnp.where(own == other, scores, MASKED)
            first = scores[:, :block]
            second = scores[:, block:]
            e_first = jnp.exp2(first - jnp.max(first, axis=-1, keepdims=True))
            e_second = jnp.exp2(second - jnp.max(second, axis=-1, keepdims=True))
            weights = jnp.concatenate([e_first, e_second], axis=1).astype(BF16)
            r_first = 1.0 / jnp.sum(e_first, axis=-1, keepdims=True)
            r_second = 1.0 / jnp.sum(e_second, axis=-1, keepdims=True)
            result = dot(weights, vals2) * jnp.where(low[:count], r_first, r_second)
            out[start : start + count, at + pair * LANES : at + (pair + 1) * LANES] = result.astype(BF16)


def temporal_heads(x, w_ref, att_ref, frames, waits=None):
    made = []
    for member in range(3):
        if waits:
            waits[member].wait()
        flat = dot(x, w_ref[member])
        made.append((flat * SCALE if member == 0 else flat).astype(BF16))
    temporal_pairs(*made, att_ref, 0, frames)


def own_heads_kernel(a_ref, w_ref, x_out, att_out, held, w_held, sems):
    copies = [pltpu.make_async_copy(a_ref, held, sems.at[3])]
    copies += [pltpu.make_async_copy(w_ref.at[i], w_held.at[i], sems.at[i]) for i in range(3)]
    for copy in copies:
        copy.start()
    copies[0].wait()
    frames = held.shape[0]
    main, extra = load_packed(held)
    size = main.shape[0]
    row = iota((size, size), 0)
    col = iota((size, size), 1)
    swap = jnp.where((row % frames) * ROWS + row // frames == col, 1.0, 0.0).astype(BF16)
    x = jnp.concatenate([dot(swap, main).astype(BF16), extra], axis=0)
    x_out[...] = x
    temporal_heads(x, w_held, att_out, frames, copies[1:])


def other_heads_kernel(count, x_ref, own_ref, *refs):
    pieces = refs[:count]
    out_ref, w_held, att_ref, sems = refs[count:]
    copies = piece_copies(pieces, part_starts(pieces[0].shape[1], pieces[4].shape[1]), w_held, sems)
    for copy in copies:
        copy.start()
    frames = out_ref.shape[0]
    size = frames * ROWS
    row = iota((size, size), 0)
    col = iota((size, size), 1)
    back = jnp.where((row % ROWS) * frames + row // ROWS == col, 1.0, 0.0).astype(BF16)
    for copy in copies:
        copy.wait()
    temporal_heads(x_ref[...], w_held, att_ref, frames)
    both = jnp.concatenate([own_ref[...], att_ref[...]], axis=1)
    store_packed(out_ref, dot(back, both[:size]), both[size:])


def join_kernel(*refs):
    *pieces, out_ref, sems = refs
    copies = piece_copies(pieces, quarter_starts(out_ref.shape[0] // 4), out_ref, sems)
    for copy in copies:
        copy.start()
    for copy in copies:
        copy.wait()


def middle_kernel(mine, r_ref, x_ref, own_ref, other_ref, gain_ref, w_ref, mid_ref, qkv_ref, held, sem):
    half = held.shape[0]
    copy = pltpu.make_async_copy(x_ref.at[half_rows(half, mine), :], held, sem)
    copy.start()
    main, extra = load_packed(r_ref)
    att = jnp.concatenate([main, extra], axis=0)
    local = own_ref.shape[0]
    first, second = (own_ref, other_ref) if mine else (other_ref, own_ref)
    summed = dot(att[:, :local], first[...]) + dot(att[:, local:], second[...])
    copy.wait()
    mid = (held[...].astype(F32) + summed).astype(BF16)
    mid_ref[...] = mid
    normed = layer_norm(mid.astype(F32), gain_ref[...])
    qkv_ref[0] = (dot(normed, w_ref[0]) * SCALE).astype(BF16)
    qkv_ref[1] = dot(normed, w_ref[1]).astype(BF16)
    qkv_ref[2] = dot(normed, w_ref[2]).astype(BF16)


def spatial_kernel(first, last, own_ref, other_ref, out_ref):
    half = own_ref.shape[1]
    low = iota((2 * half, LANES), 1) < HD
    for pair in range(first, last):
        lanes = slice(pair * LANES, (pair + 1) * LANES)
        keys = jnp.concatenate([own_ref[1, :, lanes], other_ref[1, :, lanes]], axis=0)
        vals = jnp.concatenate([own_ref[2, :, lanes], other_ref[2, :, lanes]], axis=0)
        zero = jnp.zeros_like(keys)
        one = jnp.ones_like(keys)
        keys_of = (jnp.where(low, keys, zero), jnp.where(low, zero, keys))
        vals_of = (jnp.where(low, vals, one), jnp.where(low, one, vals))
        for part, ref in enumerate((own_ref, other_ref)):
            q = ref[0, :, lanes]
            results = []
            for head in range(2):
                scores = dot_t(q, keys_of[head])
                weights = jnp.exp2(scores - jnp.max(scores, axis=-1, keepdims=True)).astype(BF16)
                results.append(dot(weights, vals_of[head]))
            here = low[:half]
            top = jnp.where(here, results[0], results[1])
            bottom = pltpu.roll(jnp.where(here, results[1], results[0]), HD, 1)
            at = (pair - first) * LANES
            out_ref[part * half : (part + 1) * half, at : at + LANES] = (top / bottom).astype(BF16)


def early_kernel(chunks, *refs):
    mids = refs[:2]
    own = refs[2 : 2 + chunks]
    own_ref, out_ref = refs[2 + chunks :]
    half = mids[0].shape[0]
    for part in range(2):
        here = slice(part * half, (part + 1) * half)
        left = jnp.concatenate([ref[here, :] for ref in own], axis=1)
        out_ref[here, :] = mids[part][...].astype(F32) + dot(left, own_ref[...])


def add_kernel(first, last, total_ref, partner, other_ref, out_ref):
    half = total_ref.shape[0] // 2
    width = partner.shape[1]
    for part, mine in enumerate((True, False)):
        here = slice(part * half, (part + 1) * half)
        there = slice((1 - part) * half, (2 - part) * half)
        total = total_ref[here, :] + dot(partner[there, :], other_ref[first : first + width, :])
        if last:
            out_ref[half_rows(half, mine), :] = total.astype(BF16)
        else:
            out_ref[here, :] = total


def call(kernel, out, places, scratch=(), us=0, limit=24, spots=None):
    spaces = {"a": pltpu.HBM, "v": pltpu.VMEM}
    many = isinstance(out, tuple)
    spots = spots or "v" * (len(out) if many else 1)
    spots = [pl.BlockSpec(memory_space=spaces[spot]) for spot in spots]
    return pl.pallas_call(
        kernel,
        out_shape=out,
        in_specs=[pl.BlockSpec(memory_space=spaces[place]) for place in places],
        out_specs=tuple(spots) if many else spots[0],
        scratch_shapes=list(scratch),
        compiler_params=pltpu.CompilerParams(vmem_limit_bytes=limit * 1024 * 1024),
        cost_estimate=pl.CostEstimate(
            flops=int(us * 1000000000), bytes_accessed=1000000, transcendentals=0
        ),
    )


def shape(*dims, dtype=BF16):
    return jax.ShapeDtypeStruct(dims, dtype)


def routes():
    devices = [(y, c, m) for y in (0, 1) for c in (0, 1) for m in (0, 1)]

    def index(y, c, m):
        return y * 4 + c * 2 + m

    across = [(index(y, c, m), index(1 - y, c, 1 - m)) for y, c, m in devices]
    beside = [(index(y, c, m), index(1 - y, c, m)) for y, c, m in devices]
    core = [(index(y, c, m), index(y, 1 - c, m)) for y, c, m in devices]
    return across, beside, core


def fetch(piece):
    return lax.ppermute(piece, ("clip", "mp"), routes()[0])


def to_beside(piece):
    return lax.ppermute(piece, ("clip", "mp"), routes()[1])


def to_core(piece):
    return lax.ppermute(piece, ("clip", "mp"), routes()[2])


def share_quarters(mine):
    chip = to_beside(mine)
    return [mine, to_core(mine), chip, to_core(chip)]


def share_parts(first, second):
    chip = to_beside(first)
    return [first, to_core(first), chip, to_core(chip), second, to_core(second)]


def all_to_all(values):
    return lax.all_to_all(values, "tm", split_axis=0, concat_axis=0, tiled=True)


def shards(video, gain_time, qkv_time, proj_time, gain_space, qkv_space, proj_space):
    _, patches, width = video.shape
    frames = lax.axis_size("tm")
    local = qkv_time.shape[-1]
    half = patches // 2
    x = video[0]
    w_time = jnp.transpose(qkv_time, (1, 0, 2))
    w_space = jnp.transpose(qkv_space, (1, 0, 2))
    gain_time = gain_time.reshape(1, width)
    gain_space = gain_space.reshape(1, width)
    packed = shape(frames, ROWS, width + LANES)
    dma = pltpu.SemaphoreType.DMA

    quarter = local // 4
    rows = width // 64 * 10
    rest = width // 2 - 2 * rows
    kept = [
        pltpu.with_memory_space_constraint(value, pltpu.HBM)
        for value in (x, gain_time, w_time, proj_time, proj_space)
    ]
    first = fetch(call(cut_kernel, shape(3, rows, local), "a", [dma])(kept[2]))
    sent, second = call(
        norm_kernel,
        (packed, shape(3, rest, local)),
        "aaa",
        [pltpu.VMEM((half, width), BF16), pltpu.VMEM((1, width), F32), dma((3,))],
        us=C_NORM,
    )(*kept[:3])
    second = fetch(second)
    pieces = share_parts(first, second)
    time_piece, space_piece = call(
        cut_proj_kernel, (shape(quarter, width), shape(quarter, width)), "aa", [dma((2,))]
    )(*kept[3:])
    time_piece, space_piece = fetch(time_piece), fetch(space_piece)
    arrived = all_to_all(sent)

    normed, att_own = call(
        own_heads_kernel,
        (shape(half, width), shape(half, local)),
        "aa",
        [packed_scratch(packed), pltpu.VMEM((3, width, local), BF16), dma((4,))],
        us=0,
    )(arrived, kept[2])
    attended = call(
        functools.partial(other_heads_kernel, len(pieces)),
        packed,
        "vv" + "a" * len(pieces),
        [pltpu.VMEM((3, width, local), BF16), pltpu.VMEM((half, local), BF16), dma((len(pieces),))],
    )(normed, att_own, *pieces)
    back = all_to_all(attended)

    time_pieces = share_quarters(time_piece)
    space_pieces = share_quarters(space_piece)
    other_time, other_space = [
        call(join_kernel, shape(local, width), "aaaa", [dma((4,))], us=cost)(*parts)
        for parts, cost in ((time_pieces, C_JOIN), (space_pieces, 0))
    ]
    theirs = lax.ppermute(back, "mp", [(0, 1), (1, 0)])
    theirs, other_space = lax.optimization_barrier((theirs, other_space))
    made = []
    for mine, values in ((True, back), (False, theirs)):
        made.append(
            call(
                functools.partial(middle_kernel, mine),
                (shape(half, width), shape(3, half, local)),
                "vavvvv",
                [pltpu.VMEM((half, width), BF16), dma],
            )(values, x, proj_time, other_time, gain_space, w_space)
        )
    (mid_own, qkv_own), (mid_other, qkv_other) = made

    own, partner = [], []
    pairs = local // LANES
    step = 1
    for first in range(0, pairs, step):
        part = call(
            functools.partial(spatial_kernel, first, first + step),
            shape(patches, step * LANES),
            "vv",
        )(qkv_own, qkv_other)
        own.append(part)
        partner.append(lax.ppermute(part, "mp", [(0, 1), (1, 0)]))
    chunks = len(own)
    total = call(
        functools.partial(early_kernel, chunks),
        shape(patches, width, dtype=F32),
        "v" * (2 + chunks + 1),
    )(mid_own, mid_other, *own, proj_space)
    for at, part in enumerate(partner):
        last = at == chunks - 1
        total = call(
            functools.partial(add_kernel, at * step * LANES, last),
            shape(patches, width, dtype=BF16 if last else F32),
            "vvv",
        )(total, part, other_space)
    return total[None]


def packed_scratch(packed):
    return pltpu.VMEM(packed.shape, packed.dtype)


def solution(mesh):
    placed = (
        P(("clip", "tm"), None, None),
        P(),
        P(None, None, "mp"),
        P("mp", None),
        P(),
        P(None, None, "mp"),
        P("mp", None),
    )
    return jax.shard_map(
        shards, mesh=mesh, in_specs=placed, out_specs=P(("clip", "tm"), None, None), check_vma=False
    )
```

```python
import functools
import math

import jax
import jax.numpy as jnp
from jax import lax
from jax.experimental import pallas as pl
from jax.experimental.pallas import tpu as pltpu
from jax.sharding import PartitionSpec as P

HD = 64
LANES = 128
ROWS = 8
F32 = jnp.float32
BF16 = jnp.bfloat16
SCALE = math.log2(math.e) / math.sqrt(HD)
EPS = 1e-05
MASKED = -1e30
C_JOIN = 1


def dot(left, right):
    return jnp.dot(left, right, preferred_element_type=F32)


def dot_t(left, right):
    return lax.dot_general(left, right, (((1,), (1,)), ((), ())), preferred_element_type=F32)


def iota(shape, dim):
    return lax.broadcasted_iota(jnp.int32, shape, dim)


def layer_norm(wide, gain):
    center = jnp.mean(wide, axis=-1, keepdims=True)
    moved = wide - center
    spread = jnp.mean(moved * moved, axis=-1, keepdims=True)
    return (moved * lax.rsqrt(spread + EPS) * gain).astype(BF16)


def spread_rows(rows):
    n, width = rows.shape
    groups = width // LANES
    at = iota((n * groups, n), 0)
    row = iota((n * groups, n), 1)
    total = jnp.zeros((n * groups, LANES), F32)
    for group in range(groups):
        pick = jnp.where(at == row * groups + group, 1.0, 0.0).astype(BF16)
        total = total + dot(pick, rows[:, group * LANES : (group + 1) * LANES])
    return total


def gather_rows(spread, groups):
    n = spread.shape[0] // groups
    row = iota((n, n * groups), 0)
    at = iota((n, n * groups), 1)
    parts = []
    for group in range(groups):
        pick = jnp.where(at == row * groups + group, 1.0, 0.0).astype(BF16)
        parts.append(dot(pick, spread).astype(BF16))
    return jnp.concatenate(parts, axis=1)


def store_packed(out_ref, main, extra):
    n, rows, _ = out_ref.shape
    width = main.shape[1]
    out_ref[:, :, :width] = main.reshape(n, rows, width).astype(BF16)
    out_ref[:, :, width:] = spread_rows(extra).reshape(n, rows, LANES).astype(BF16)


def load_packed(ref):
    n, rows, full = ref.shape
    width = full - LANES
    main = ref[:, :, :width].astype(F32).reshape(n * rows, width).astype(BF16)
    tail = ref[:, :, width:].astype(F32).reshape(n * rows, LANES).astype(BF16)
    return main, gather_rows(tail, rows)


def half_rows(count, mine):
    member = lax.axis_index("mp")
    place = member if mine else 1 - member
    return pl.ds(pl.multiple_of(place * count, 32), count)


def cut_kernel(w_ref, out_ref, sem):
    rows = out_ref.shape[1]
    start = (lax.axis_index("clip") ^ 2) * rows
    copy = pltpu.make_async_copy(w_ref.at[:, pl.ds(pl.multiple_of(start, 16), rows), :], out_ref, sem)
    copy.start()
    copy.wait()


def cut_rest_kernel(w_ref, out_ref, sem):
    rows = out_ref.shape[1]
    start = w_ref.shape[1] - 2 * rows + (lax.axis_index("clip") % 2) * rows
    copy = pltpu.make_async_copy(w_ref.at[:, pl.ds(pl.multiple_of(start, 16), rows), :], out_ref, sem)
    copy.start()
    copy.wait()


def cut_more_kernel(rows, w_ref, time_ref, space_ref, mixed_ref, sems):
    clip = lax.axis_index("clip")
    place = pl.ds(pl.multiple_of((clip ^ 2) * rows, 16), rows)
    copies = [
        pltpu.make_async_copy(w_ref.at[at, place, :], mixed_ref.at[at * rows : (at + 1) * rows, :], sems.at[at])
        for at in range(3)
    ]
    quarter = time_ref.shape[0] // 4
    wide = mixed_ref.shape[1]
    place = pl.ds(pl.multiple_of((clip ^ 2) * quarter, 16), quarter)
    at = 3 * rows
    for ref in (time_ref, space_ref):
        for column in range(ref.shape[1] // wide):
            part = ref.at[place, column * wide : (column + 1) * wide]
            copies.append(pltpu.make_async_copy(part, mixed_ref.at[at : at + quarter, :], sems.at[len(copies)]))
            at += quarter
    for copy in copies:
        copy.start()
    for copy in copies:
        copy.wait()


def join_kernel(first_ref, second_ref, third_ref, fourth_ref, rest_ref, far_ref, w_ref, time_ref, space_ref, sems):
    clip = lax.axis_index("clip")
    rest = rest_ref.shape[1]
    rows = w_ref.shape[1] // 4 - rest // 2
    quarter = time_ref.shape[0] // 4
    copies = []

    def add(source, target):
        copies.append(pltpu.make_async_copy(source, target, sems.at[len(copies)]))

    for distance, ref in enumerate((first_ref, second_ref, third_ref, fourth_ref)):
        place = pl.ds(pl.multiple_of((clip ^ distance) * quarter, 16), quarter)
        wide = ref.shape[1]
        at = 3 * rows
        for target in (time_ref, space_ref):
            for column in range(target.shape[1] // wide):
                spot = target.at[place, column * wide : (column + 1) * wide]
                add(ref.at[at : at + quarter, :], spot)
                at += quarter
        place = pl.ds(pl.multiple_of((clip ^ distance) * rows, 16), rows)
        for at in range(3):
            add(ref.at[at * rows : (at + 1) * rows, :], w_ref.at[at, place, :])
    for distance, ref in enumerate((rest_ref, far_ref)):
        start = 4 * rows + ((clip % 2) ^ distance) * rest
        add(ref, w_ref.at[:, pl.ds(pl.multiple_of(start, 16), rest), :])
    for copy in copies:
        copy.start()
    for copy in copies:
        copy.wait()


def norm_kernel(x_ref, gain_ref, w_ref, out_ref, cut_ref, held, gain, sems):
    half = held.shape[0]
    main = out_ref.shape[0] * ROWS
    rows = cut_ref.shape[1]
    start = w_ref.shape[1] - 2 * rows + (lax.axis_index("clip") % 2) * rows
    place = pl.ds(pl.multiple_of(start, 16), rows)
    copies = [
        pltpu.make_async_copy(x_ref.at[half_rows(half, True), :], held, sems.at[0]),
        pltpu.make_async_copy(gain_ref, gain, sems.at[1]),
        pltpu.make_async_copy(w_ref.at[:, place, :], cut_ref, sems.at[2]),
    ]
    for copy in copies:
        copy.start()
    copies[0].wait()
    copies[1].wait()
    normed = layer_norm(held[...].astype(F32), gain[...])
    store_packed(out_ref, normed[:main].astype(F32), normed[main:])
    copies[2].wait()


def piece_copies(pieces, starts, target, sems):
    copies = []
    for at, (piece, start) in enumerate(zip(pieces, starts, strict=True)):
        place = pl.ds(pl.multiple_of(start, 16), piece.shape[-2])
        spot = target.at[:, place, :] if len(target.shape) == 3 else target.at[place, :]
        copies.append(pltpu.make_async_copy(piece, spot, sems.at[at]))
    return copies


def part_starts(first, second):
    clip = lax.axis_index("clip")
    starts = [(clip ^ distance) * first for distance in range(4)]
    return starts + [4 * first + ((clip % 2) ^ distance) * second for distance in range(2)]


def two_heads(keys, vals):
    low = iota(keys.shape, 1) < HD
    zero = jnp.zeros_like(keys)
    one = jnp.ones_like(keys)
    keys2 = jnp.concatenate([jnp.where(low, keys, zero), jnp.where(low, zero, keys)], axis=0)
    first = jnp.concatenate([jnp.where(low, vals, zero), jnp.where(low, one, zero)], axis=1)
    second = jnp.concatenate([jnp.where(low, zero, vals), jnp.where(low, zero, one)], axis=1)
    return keys2, jnp.concatenate([first, second], axis=0)


def weighted(weights, vals2):
    result = dot(weights, vals2)
    return (result[:, :LANES] / result[:, LANES:]).astype(BF16)


def temporal_pairs(q, k, v, out, at, frames):
    rows = q.shape[0]
    block = 4 * frames
    for pair in range(q.shape[1] // LANES):
        lanes = slice(pair * LANES, (pair + 1) * LANES)
        for start in range(0, rows, block):
            count = min(block, rows - start)
            key_at = start + count - block
            keys2, vals2 = two_heads(k[key_at : key_at + block, lanes], v[key_at : key_at + block, lanes])
            scores = dot_t(q[start : start + count, lanes], keys2)
            own = (iota((count, 2 * block), 0) + (start - key_at)) // frames
            other = (iota((count, 2 * block), 1) % block) // frames
            scores = jnp.where(own == other, scores, MASKED)
            halves = [scores[:, :block], scores[:, block:]]
            halves = [jnp.exp2(part - jnp.max(part, axis=-1, keepdims=True)).astype(BF16) for part in halves]
            result = weighted(jnp.concatenate(halves, axis=1), vals2)
            out[start : start + count, at + pair * LANES : at + (pair + 1) * LANES] = result


def temporal_kernel(count, a_ref, own_ref, *refs):
    pieces = refs[:count]
    out_ref, att_ref, other_ref, sems = refs[count:]
    starts = part_starts(pieces[0].shape[1], pieces[4].shape[1])
    fetched = piece_copies(pieces, starts, other_ref, sems)
    for copy in fetched:
        copy.start()
    frames = a_ref.shape[0]
    local = own_ref.shape[-1]
    main, extra = load_packed(a_ref)
    size = main.shape[0]
    row = iota((size, size), 0)
    col = iota((size, size), 1)
    swap = jnp.where((row % frames) * ROWS + row // frames == col, 1.0, 0.0).astype(BF16)
    x = jnp.concatenate([dot(swap, main).astype(BF16), extra], axis=0)
    for member, weights in enumerate((own_ref, other_ref)):
        for copy in fetched if member else ():
            copy.wait()
        q = (dot(x, weights[0]) * SCALE).astype(BF16)
        k = dot(x, weights[1]).astype(BF16)
        v = dot(x, weights[2]).astype(BF16)
        temporal_pairs(q, k, v, att_ref, member * local, frames)
    back = jnp.where((row % ROWS) * frames + row // ROWS == col, 1.0, 0.0).astype(BF16)
    store_packed(out_ref, dot(back, att_ref[:size, :]), att_ref[size:, :])


def middle_kernel(mine, r_ref, x_ref, p_own, p_other, gain_ref, w_own, w_other, mid_ref, qkv_ref, held, sem):
    half = held.shape[0]
    copy = pltpu.make_async_copy(x_ref.at[half_rows(half, mine), :], held, sem)
    copy.start()
    main, extra = load_packed(r_ref)
    att = jnp.concatenate([main, extra], axis=0)
    local = p_own.shape[0]
    first, second = (p_own, p_other) if mine else (p_other, p_own)
    summed = dot(att[:, :local], first[...]) + dot(att[:, local:], second[...])
    copy.wait()
    mid = (held[...].astype(F32) + summed).astype(BF16)
    mid_ref[...] = mid
    normed = layer_norm(mid.astype(F32), gain_ref[...])
    for at, w_ref in enumerate((w_own, w_other)):
        lanes = slice(at * local, (at + 1) * local)
        qkv_ref[0, :, lanes] = (dot(normed, w_ref[0]) * SCALE).astype(BF16)
        qkv_ref[1, :, lanes] = dot(normed, w_ref[1]).astype(BF16)
        qkv_ref[2, :, lanes] = dot(normed, w_ref[2]).astype(BF16)


def spatial_kernel(own_ref, other_ref, mid_own, mid_other, p_own, p_other, out_ref, att_ref):
    half, width = mid_own.shape
    patches = 2 * half
    local = p_own.shape[0]
    split = patches // LANES * LANES
    low = iota((1, LANES), 1) < HD
    for pair in range(width // LANES):
        lanes = slice(pair * LANES, (pair + 1) * LANES)
        keys2, vals2 = two_heads(
            jnp.concatenate([own_ref[1, :, lanes], other_ref[1, :, lanes]], axis=0),
            jnp.concatenate([own_ref[2, :, lanes], other_ref[2, :, lanes]], axis=0),
        )
        for part, ref in enumerate((own_ref, other_ref)):
            scores = dot_t(ref[0, :, lanes], keys2)
            left = scores[:, :split]
            both = scores[:, split : split + LANES]
            right = scores[:, split + LANES :]
            top_left = jnp.maximum(
                jnp.max(left, axis=-1, keepdims=True),
                jnp.max(jnp.where(low, both, MASKED), axis=-1, keepdims=True),
            )
            top_right = jnp.maximum(
                jnp.max(right, axis=-1, keepdims=True),
                jnp.max(jnp.where(low, MASKED, both), axis=-1, keepdims=True),
            )
            moved = (left - top_left, both - jnp.where(low, top_left, top_right), right - top_right)
            weights = jnp.concatenate([jnp.exp2(value).astype(BF16) for value in moved], axis=1)
            att_ref[part * half : (part + 1) * half, lanes] = weighted(weights, vals2)
    for part, (mine, mid) in enumerate(((True, mid_own), (False, mid_other))):
        here = slice(part * half, (part + 1) * half)
        total = mid[...].astype(F32) + dot(att_ref[here, :local], p_own[...])
        total = total + dot(att_ref[here, local:], p_other[...])
        out_ref[half_rows(half, mine), :] = total.astype(BF16)


def call(kernel, out, places, scratch=(), us=0, limit=24, spots=None):
    spaces = {"a": pl.ANY, "v": pltpu.VMEM}
    many = isinstance(out, tuple)
    spots = spots or "v" * (len(out) if many else 1)
    spots = [pl.BlockSpec(memory_space=spaces[spot]) for spot in spots]
    return pl.pallas_call(
        kernel,
        out_shape=out,
        in_specs=[pl.BlockSpec(memory_space=spaces[place]) for place in places],
        out_specs=tuple(spots) if many else spots[0],
        scratch_shapes=list(scratch),
        compiler_params=pltpu.CompilerParams(vmem_limit_bytes=limit * 1024 * 1024),
        cost_estimate=pl.CostEstimate(
            flops=int(us * 1000000000), bytes_accessed=1000000, transcendentals=0
        ),
    )


def shape(*dims, dtype=BF16):
    return jax.ShapeDtypeStruct(dims, dtype)


def routes():
    devices = [(y, c, m) for y in (0, 1) for c in (0, 1) for m in (0, 1)]

    def index(y, c, m):
        return y * 4 + c * 2 + m

    across = [(index(y, c, m), index(1 - y, c, 1 - m)) for y, c, m in devices]
    beside = [(index(y, c, m), index(1 - y, c, m)) for y, c, m in devices]
    core = [(index(y, c, m), index(y, 1 - c, m)) for y, c, m in devices]
    return across, beside, core


def fetch(piece):
    return lax.ppermute(piece, ("clip", "mp"), routes()[0])


def to_beside(piece):
    return lax.ppermute(piece, ("clip", "mp"), routes()[1])


def to_core(piece):
    return lax.ppermute(piece, ("clip", "mp"), routes()[2])


def share_parts(first, second):
    chip = to_beside(first)
    return [first, to_core(first), chip, to_core(chip), second, to_core(second)]


def all_to_all(values):
    return lax.all_to_all(values, "tm", split_axis=0, concat_axis=0, tiled=True)


def in_hbm(value):
    return pltpu.with_memory_space_constraint(value, pltpu.HBM)


def in_vmem(value):
    return pltpu.with_memory_space_constraint(value, pltpu.VMEM)


def shards(video, gain_time, qkv_time, proj_time, gain_space, qkv_space, proj_space):
    _, patches, width = video.shape
    frames = lax.axis_size("tm")
    local = qkv_time.shape[-1]
    half = patches // 2
    x = video[0]
    w_time = jnp.transpose(qkv_time, (1, 0, 2))
    w_space = jnp.transpose(qkv_space, (1, 0, 2))
    gain_time = gain_time.reshape(1, width)
    gain_space = gain_space.reshape(1, width)
    packed = shape(frames, ROWS, width + LANES)
    dma = pltpu.SemaphoreType.DMA

    rows = width // 64 * 10
    rest = width // 2 - 2 * rows
    first = fetch(call(cut_kernel, shape(3, rows, local), "a", [dma])(in_hbm(w_time)))
    sent, second = call(
        norm_kernel,
        (packed, shape(3, rest, local)),
        "aaa",
        [pltpu.VMEM((half, width), BF16), pltpu.VMEM((1, width), F32), dma((3,))],
    )(in_hbm(x), in_hbm(gain_time), in_hbm(w_time))
    first, w_space_, proj_time_, proj_space_ = lax.optimization_barrier((first, w_space, proj_time, proj_space))
    second, w_late = lax.optimization_barrier((fetch(second), w_space_))
    pieces = share_parts(first, second)
    arrived = all_to_all(sent)
    held = pltpu.VMEM(w_time.shape, BF16)
    attended = call(
        functools.partial(temporal_kernel, len(pieces)),
        packed,
        "vv" + "a" * len(pieces),
        [pltpu.VMEM((half, width), BF16), held, dma((len(pieces),))],
    )(arrived, w_time, *[in_hbm(p) for p in pieces])
    back = all_to_all(attended)

    quarter = local // 4
    rows = width // 64 * 6
    rest = width // 2 - 2 * rows
    height = 3 * rows + 4 * quarter
    mixed = call(functools.partial(cut_more_kernel, rows), shape(height, local), "aaa", [dma((7,))])(
        in_hbm(w_space_), in_hbm(proj_time_), in_hbm(proj_space_)
    )
    far = call(cut_rest_kernel, shape(3, rest, local), "a", [dma])(in_hbm(w_late))
    mixed, _ = lax.optimization_barrier((fetch(mixed), attended))
    more = share_parts(mixed, fetch(far))
    space_other, other_time, other_space = call(
        join_kernel,
        (pltpu.VMEM(w_space.shape, BF16), shape(local, width), shape(local, width)),
        "aaaaaa",
        [dma((30,))],
        us=C_JOIN,
    )(*more)

    theirs = lax.ppermute(back, "mp", [(0, 1), (1, 0)])
    made = []
    for mine, values in ((True, back), (False, theirs)):
        made.append(
            call(
                functools.partial(middle_kernel, mine),
                (shape(half, width), shape(3, half, width)),
                "vavvvvv",
                [pltpu.VMEM((half, width), BF16), dma],
            )(values, x, proj_time, other_time, gain_space, w_space, in_vmem(space_other))
        )
    (mid_own, qkv_own), (mid_other, qkv_other) = made
    out = call(spatial_kernel, shape(patches, width), "vvvvvv", [pltpu.VMEM((patches, width), BF16)])(
        qkv_own, qkv_other, mid_own, mid_other, proj_space, other_space
    )
    return out[None]


def solution(mesh):
    placed = (
        P(("clip", "tm"), None, None),
        P(),
        P(None, None, "mp"),
        P("mp", None),
        P(),
        P(None, None, "mp"),
        P("mp", None),
    )
    return jax.shard_map(
        shards, mesh=mesh, in_specs=placed, out_specs=P(("clip", "tm"), None, None), check_vma=False
    )
```

```python
import functools
import math

import jax
import jax.numpy as jnp
from jax import lax
from jax.experimental import pallas as pl
from jax.experimental.pallas import tpu as pltpu
from jax.sharding import PartitionSpec as P

HD = 64
LANES = 128
ROWS = 8
F32 = jnp.float32
BF16 = jnp.bfloat16
SCALE = math.log2(math.e) / math.sqrt(HD)
EPS = 1e-05
MASKED = -1e30
C_JOIN = 2


def dot(left, right):
    return jnp.dot(left, right, preferred_element_type=F32)


def dot_t(left, right):
    return lax.dot_general(left, right, (((1,), (1,)), ((), ())), preferred_element_type=F32)


def iota(shape, dim):
    return lax.broadcasted_iota(jnp.int32, shape, dim)


def layer_norm(wide, gain):
    center = jnp.mean(wide, axis=-1, keepdims=True)
    moved = wide - center
    spread = jnp.mean(moved * moved, axis=-1, keepdims=True)
    return (moved * lax.rsqrt(spread + EPS) * gain).astype(BF16)


def spread_rows(rows):
    n, width = rows.shape
    groups = width // LANES
    at = iota((n * groups, n), 0)
    row = iota((n * groups, n), 1)
    total = jnp.zeros((n * groups, LANES), F32)
    for group in range(groups):
        pick = jnp.where(at == row * groups + group, 1.0, 0.0).astype(BF16)
        total = total + dot(pick, rows[:, group * LANES : (group + 1) * LANES])
    return total


def gather_rows(spread, groups):
    n = spread.shape[0] // groups
    row = iota((n, n * groups), 0)
    at = iota((n, n * groups), 1)
    parts = []
    for group in range(groups):
        pick = jnp.where(at == row * groups + group, 1.0, 0.0).astype(BF16)
        parts.append(dot(pick, spread).astype(BF16))
    return jnp.concatenate(parts, axis=1)


def store_packed(out_ref, main, extra):
    n, rows, _ = out_ref.shape
    width = main.shape[1]
    out_ref[:, :, :width] = main.reshape(n, rows, width).astype(BF16)
    out_ref[:, :, width:] = spread_rows(extra).reshape(n, rows, LANES).astype(BF16)


def load_packed(ref):
    n, rows, full = ref.shape
    width = full - LANES
    main = ref[:, :, :width].astype(F32).reshape(n * rows, width).astype(BF16)
    tail = ref[:, :, width:].astype(F32).reshape(n * rows, LANES).astype(BF16)
    return main, gather_rows(tail, rows)


def half_rows(count, mine):
    member = lax.axis_index("mp")
    place = member if mine else 1 - member
    return pl.ds(pl.multiple_of(place * count, 32), count)


def cut_kernel(w_ref, out_ref, sem):
    rows = out_ref.shape[1]
    start = (lax.axis_index("clip") ^ 2) * rows
    copy = pltpu.make_async_copy(w_ref.at[:, pl.ds(pl.multiple_of(start, 16), rows), :], out_ref, sem)
    copy.start()
    copy.wait()


def cut_rest_kernel(w_ref, out_ref, sem):
    rows = out_ref.shape[1]
    start = w_ref.shape[1] - 2 * rows + (lax.axis_index("clip") % 2) * rows
    copy = pltpu.make_async_copy(w_ref.at[:, pl.ds(pl.multiple_of(start, 16), rows), :], out_ref, sem)
    copy.start()
    copy.wait()


def cut_more_kernel(rows, w_ref, time_ref, space_ref, mixed_ref, sems):
    clip = lax.axis_index("clip")
    place = pl.ds(pl.multiple_of((clip ^ 2) * rows, 16), rows)
    copies = [
        pltpu.make_async_copy(w_ref.at[at, place, :], mixed_ref.at[at * rows : (at + 1) * rows, :], sems.at[at])
        for at in range(3)
    ]
    quarter = time_ref.shape[0] // 4
    wide = mixed_ref.shape[1]
    place = pl.ds(pl.multiple_of((clip ^ 2) * quarter, 16), quarter)
    at = 3 * rows
    for ref in (time_ref, space_ref):
        for column in range(ref.shape[1] // wide):
            part = ref.at[place, column * wide : (column + 1) * wide]
            copies.append(pltpu.make_async_copy(part, mixed_ref.at[at : at + quarter, :], sems.at[len(copies)]))
            at += quarter
    for copy in copies:
        copy.start()
    for copy in copies:
        copy.wait()


def join_kernel(first_ref, second_ref, third_ref, fourth_ref, rest_ref, far_ref, w_ref, time_ref, space_ref, sems):
    clip = lax.axis_index("clip")
    rest = rest_ref.shape[1]
    rows = w_ref.shape[1] // 4 - rest // 2
    quarter = time_ref.shape[0] // 4
    copies = []

    def add(source, target):
        copies.append(pltpu.make_async_copy(source, target, sems.at[len(copies)]))

    for distance, ref in enumerate((first_ref, second_ref, third_ref, fourth_ref)):
        place = pl.ds(pl.multiple_of((clip ^ distance) * quarter, 16), quarter)
        wide = ref.shape[1]
        at = 3 * rows
        for target in (time_ref, space_ref):
            for column in range(target.shape[1] // wide):
                spot = target.at[place, column * wide : (column + 1) * wide]
                add(ref.at[at : at + quarter, :], spot)
                at += quarter
        place = pl.ds(pl.multiple_of((clip ^ distance) * rows, 16), rows)
        for at in range(3):
            add(ref.at[at * rows : (at + 1) * rows, :], w_ref.at[at, place, :])
    for distance, ref in enumerate((rest_ref, far_ref)):
        start = 4 * rows + ((clip % 2) ^ distance) * rest
        add(ref, w_ref.at[:, pl.ds(pl.multiple_of(start, 16), rest), :])
    for copy in copies:
        copy.start()
    for copy in copies:
        copy.wait()


def norm_kernel(x_ref, gain_ref, w_ref, out_ref, cut_ref, held, gain, sems):
    half = held.shape[0]
    main = out_ref.shape[0] * ROWS
    rows = cut_ref.shape[1]
    start = w_ref.shape[1] - 2 * rows + (lax.axis_index("clip") % 2) * rows
    place = pl.ds(pl.multiple_of(start, 16), rows)
    copies = [
        pltpu.make_async_copy(x_ref.at[half_rows(half, True), :], held, sems.at[0]),
        pltpu.make_async_copy(gain_ref, gain, sems.at[1]),
        pltpu.make_async_copy(w_ref.at[:, place, :], cut_ref, sems.at[2]),
    ]
    for copy in copies:
        copy.start()
    copies[0].wait()
    copies[1].wait()
    normed = layer_norm(held[...].astype(F32), gain[...])
    store_packed(out_ref, normed[:main].astype(F32), normed[main:])
    copies[2].wait()


def piece_copies(pieces, starts, target, sems):
    copies = []
    for at, (piece, start) in enumerate(zip(pieces, starts, strict=True)):
        place = pl.ds(pl.multiple_of(start, 16), piece.shape[-2])
        spot = target.at[:, place, :] if len(target.shape) == 3 else target.at[place, :]
        copies.append(pltpu.make_async_copy(piece, spot, sems.at[at]))
    return copies


def part_starts(first, second):
    clip = lax.axis_index("clip")
    starts = [(clip ^ distance) * first for distance in range(4)]
    return starts + [4 * first + ((clip % 2) ^ distance) * second for distance in range(2)]


def two_heads(keys, vals):
    low = iota(keys.shape, 1) < HD
    zero = jnp.zeros_like(keys)
    one = jnp.ones_like(keys)
    keys2 = jnp.concatenate([jnp.where(low, keys, zero), jnp.where(low, zero, keys)], axis=0)
    first = jnp.concatenate([jnp.where(low, vals, zero), jnp.where(low, one, zero)], axis=1)
    second = jnp.concatenate([jnp.where(low, zero, vals), jnp.where(low, zero, one)], axis=1)
    return keys2, jnp.concatenate([first, second], axis=0)


def weighted(weights, vals2):
    result = dot(weights, vals2)
    return (result[:, :LANES] / result[:, LANES:]).astype(BF16)


def temporal_pairs(q, k, v, out, at, frames):
    rows = q.shape[0]
    block = 4 * frames
    for pair in range(q.shape[1] // LANES):
        lanes = slice(pair * LANES, (pair + 1) * LANES)
        for start in range(0, rows, block):
            count = min(block, rows - start)
            key_at = start + count - block
            keys2, vals2 = two_heads(k[key_at : key_at + block, lanes], v[key_at : key_at + block, lanes])
            scores = dot_t(q[start : start + count, lanes], keys2)
            own = (iota((count, 2 * block), 0) + (start - key_at)) // frames
            other = (iota((count, 2 * block), 1) % block) // frames
            scores = jnp.where(own == other, scores, MASKED)
            halves = [scores[:, :block], scores[:, block:]]
            halves = [jnp.exp2(part - jnp.max(part, axis=-1, keepdims=True)).astype(BF16) for part in halves]
            result = weighted(jnp.concatenate(halves, axis=1), vals2)
            out[start : start + count, at + pair * LANES : at + (pair + 1) * LANES] = result


def temporal_kernel(count, a_ref, own_ref, *refs):
    pieces = refs[:count]
    out_ref, held_ref, att_ref, other_ref, sems = refs[count:]
    frames = held_ref.shape[0]
    step = frames // 4
    arriving = []
    for at in range(4):
        some = slice(at * step, (at + 1) * step)
        arriving.append(pltpu.make_async_copy(a_ref.at[some], held_ref.at[some], sems.at[3, at]))
    starts = part_starts(pieces[0].shape[1], pieces[4].shape[1])
    fetched = []
    for at in range(3):
        fetched.append(piece_copies([piece.at[at] for piece in pieces], starts, other_ref.at[at], sems.at[at]))
    for copy in arriving + fetched[0] + fetched[1] + fetched[2]:
        copy.start()
    for copy in arriving:
        copy.wait()
    local = own_ref.shape[-1]
    main, extra = load_packed(held_ref)
    size = main.shape[0]
    row = iota((size, size), 0)
    col = iota((size, size), 1)
    swap = jnp.where((row % frames) * ROWS + row // frames == col, 1.0, 0.0).astype(BF16)
    x = jnp.concatenate([dot(swap, main).astype(BF16), extra], axis=0)
    for member, weights in enumerate((own_ref, other_ref)):
        made = []
        for at in range(3):
            for copy in fetched[at] if member else ():
                copy.wait()
            flat = dot(x, weights[at])
            made.append((flat if at else flat * SCALE).astype(BF16))
        temporal_pairs(*made, att_ref, member * local, frames)
    back = jnp.where((row % ROWS) * frames + row // ROWS == col, 1.0, 0.0).astype(BF16)
    store_packed(out_ref, dot(back, att_ref[:size, :]), att_ref[size:, :])


def middle_kernel(mine, r_ref, x_ref, p_own, p_other, gain_ref, w_own, w_other, mid_ref, qkv_ref, held, sem):
    half = held.shape[0]
    copy = pltpu.make_async_copy(x_ref.at[half_rows(half, mine), :], held, sem)
    copy.start()
    main, extra = load_packed(r_ref)
    att = jnp.concatenate([main, extra], axis=0)
    local = p_own.shape[0]
    first, second = (p_own, p_other) if mine else (p_other, p_own)
    summed = dot(att[:, :local], first[...]) + dot(att[:, local:], second[...])
    copy.wait()
    mid = (held[...].astype(F32) + summed).astype(BF16)
    mid_ref[...] = mid
    normed = layer_norm(mid.astype(F32), gain_ref[...])
    for at, w_ref in enumerate((w_own, w_other)):
        lanes = slice(at * local, (at + 1) * local)
        qkv_ref[0, :, lanes] = (dot(normed, w_ref[0]) * SCALE).astype(BF16)
        qkv_ref[1, :, lanes] = dot(normed, w_ref[1]).astype(BF16)
        qkv_ref[2, :, lanes] = dot(normed, w_ref[2]).astype(BF16)


def spatial_kernel(own_ref, other_ref, mid_own, mid_other, p_own, p_other, out_ref, att_ref):
    half, width = mid_own.shape
    patches = 2 * half
    local = p_own.shape[0]
    split = patches // LANES * LANES
    low = iota((1, LANES), 1) < HD
    for pair in range(width // LANES):
        lanes = slice(pair * LANES, (pair + 1) * LANES)
        keys2, vals2 = two_heads(
            jnp.concatenate([own_ref[1, :, lanes], other_ref[1, :, lanes]], axis=0),
            jnp.concatenate([own_ref[2, :, lanes], other_ref[2, :, lanes]], axis=0),
        )
        for part, ref in enumerate((own_ref, other_ref)):
            scores = dot_t(ref[0, :, lanes], keys2)
            left = scores[:, :split]
            both = scores[:, split : split + LANES]
            right = scores[:, split + LANES :]
            top_left = jnp.maximum(
                jnp.max(left, axis=-1, keepdims=True),
                jnp.max(jnp.where(low, both, MASKED), axis=-1, keepdims=True),
            )
            top_right = jnp.maximum(
                jnp.max(right, axis=-1, keepdims=True),
                jnp.max(jnp.where(low, MASKED, both), axis=-1, keepdims=True),
            )
            moved = (left - top_left, both - jnp.where(low, top_left, top_right), right - top_right)
            weights = jnp.concatenate([jnp.exp2(value).astype(BF16) for value in moved], axis=1)
            att_ref[part * half : (part + 1) * half, lanes] = weighted(weights, vals2)
    for part, (mine, mid) in enumerate(((True, mid_own), (False, mid_other))):
        here = slice(part * half, (part + 1) * half)
        total = mid[...].astype(F32) + dot(att_ref[here, :local], p_own[...])
        total = total + dot(att_ref[here, local:], p_other[...])
        out_ref[half_rows(half, mine), :] = total.astype(BF16)


def call(kernel, out, places, scratch=(), us=0, limit=24, spots=None):
    spaces = {"a": pl.ANY, "v": pltpu.VMEM}
    many = isinstance(out, tuple)
    spots = spots or "v" * (len(out) if many else 1)
    spots = [pl.BlockSpec(memory_space=spaces[spot]) for spot in spots]
    return pl.pallas_call(
        kernel,
        out_shape=out,
        in_specs=[pl.BlockSpec(memory_space=spaces[place]) for place in places],
        out_specs=tuple(spots) if many else spots[0],
        scratch_shapes=list(scratch),
        compiler_params=pltpu.CompilerParams(vmem_limit_bytes=limit * 1024 * 1024),
        cost_estimate=pl.CostEstimate(
            flops=int(us * 1000000000), bytes_accessed=1000000, transcendentals=0
        ),
    )


def shape(*dims, dtype=BF16):
    return jax.ShapeDtypeStruct(dims, dtype)


def routes():
    devices = [(y, c, m) for y in (0, 1) for c in (0, 1) for m in (0, 1)]

    def index(y, c, m):
        return y * 4 + c * 2 + m

    across = [(index(y, c, m), index(1 - y, c, 1 - m)) for y, c, m in devices]
    beside = [(index(y, c, m), index(1 - y, c, m)) for y, c, m in devices]
    core = [(index(y, c, m), index(y, 1 - c, m)) for y, c, m in devices]
    return across, beside, core


def fetch(piece):
    return lax.ppermute(piece, ("clip", "mp"), routes()[0])


def to_beside(piece):
    return lax.ppermute(piece, ("clip", "mp"), routes()[1])


def to_core(piece):
    return lax.ppermute(piece, ("clip", "mp"), routes()[2])


def share_parts(first, second):
    chip = to_beside(first)
    return [first, to_core(first), chip, to_core(chip), second, to_core(second)]


def all_to_all(values):
    return lax.all_to_all(values, "tm", split_axis=0, concat_axis=0, tiled=True)


def in_hbm(value):
    return pltpu.with_memory_space_constraint(value, pltpu.HBM)


def in_vmem(value):
    return pltpu.with_memory_space_constraint(value, pltpu.VMEM)


def shards(video, gain_time, qkv_time, proj_time, gain_space, qkv_space, proj_space):
    _, patches, width = video.shape
    frames = lax.axis_size("tm")
    local = qkv_time.shape[-1]
    half = patches // 2
    x = video[0]
    w_time = jnp.transpose(qkv_time, (1, 0, 2))
    w_space = jnp.transpose(qkv_space, (1, 0, 2))
    gain_time = gain_time.reshape(1, width)
    gain_space = gain_space.reshape(1, width)
    packed = shape(frames, ROWS, width + LANES)
    dma = pltpu.SemaphoreType.DMA

    rows = width // 64 * 10
    rest = width // 2 - 2 * rows
    first = fetch(call(cut_kernel, shape(3, rows, local), "a", [dma])(in_hbm(w_time)))
    sent, second = call(
        norm_kernel,
        (packed, shape(3, rest, local)),
        "aaa",
        [pltpu.VMEM((half, width), BF16), pltpu.VMEM((1, width), F32), dma((3,))],
    )(in_hbm(x), in_hbm(gain_time), in_hbm(w_time))
    first, w_space_, proj_time_, proj_space_ = lax.optimization_barrier((first, w_space, proj_time, proj_space))
    second, w_late = lax.optimization_barrier((fetch(second), w_space_))
    pieces = share_parts(first, second)
    arrived = all_to_all(sent)
    held = pltpu.VMEM(w_time.shape, BF16)
    attended = call(
        functools.partial(temporal_kernel, len(pieces)),
        packed,
        "av" + "a" * len(pieces),
        [pltpu.VMEM(packed.shape, BF16), pltpu.VMEM((half, width), BF16), held, dma((4, len(pieces)))],
    )(in_hbm(arrived), w_time, *[in_hbm(p) for p in pieces])
    back = all_to_all(attended)

    quarter = local // 4
    rows = width // 64 * 6
    rest = width // 2 - 2 * rows
    height = 3 * rows + 4 * quarter
    mixed = call(functools.partial(cut_more_kernel, rows), shape(height, local), "aaa", [dma((7,))])(
        in_hbm(w_space_), in_hbm(proj_time_), in_hbm(proj_space_)
    )
    far = call(cut_rest_kernel, shape(3, rest, local), "a", [dma])(in_hbm(w_late))
    mixed, _ = lax.optimization_barrier((fetch(mixed), attended))
    more = share_parts(mixed, fetch(far))
    space_other, other_time, other_space = call(
        join_kernel,
        (pltpu.VMEM(w_space.shape, BF16), shape(local, width), shape(local, width)),
        "aaaaaa",
        [dma((30,))],
        us=C_JOIN,
    )(*more)

    theirs = lax.ppermute(back, "mp", [(0, 1), (1, 0)])
    made = []
    for mine, values in ((True, back), (False, theirs)):
        made.append(
            call(
                functools.partial(middle_kernel, mine),
                (shape(half, width), shape(3, half, width)),
                "vavvvvv",
                [pltpu.VMEM((half, width), BF16), dma],
            )(values, x, proj_time, other_time, gain_space, w_space, in_vmem(space_other))
        )
    (mid_own, qkv_own), (mid_other, qkv_other) = made
    out = call(spatial_kernel, shape(patches, width), "vvvvvv", [pltpu.VMEM((patches, width), BF16)])(
        qkv_own, qkv_other, mid_own, mid_other, proj_space, other_space
    )
    return out[None]


def solution(mesh):
    placed = (
        P(("clip", "tm"), None, None),
        P(),
        P(None, None, "mp"),
        P("mp", None),
        P(),
        P(None, None, "mp"),
        P("mp", None),
    )
    return jax.shard_map(
        shards, mesh=mesh, in_specs=placed, out_specs=P(("clip", "tm"), None, None), check_vma=False
    )
```
